256 devices in a mesh: dp: 16 (over z_hi, y), seq: 16 (over x, z_lo, core).
Axes of the slice: x: 4, y: 4, z: 8 (z_hi: 4, z_lo: 2; z = z_hi * 2 + z_lo), core: 2. Of those that a mesh axis runs over, the one named last changes fastest.
Arguments:
- queries: bfloat16 [16, 2048, 2048], P('dp', 'seq'), may hold values from -12 to 12
- key_vectors: bfloat16 [16, 2304, 2048], P('dp', 'seq'), may hold values from -12 to 12
- value_vectors: bfloat16 [16, 2304, 2048], P('dp', 'seq'), may hold values from -24 to 24
- query_tangent: bfloat16 [16, 2048, 2048], P('dp', 'seq'), may hold values from -6 to 6
- key_tangent: bfloat16 [16, 2304, 2048], P('dp', 'seq'), may hold values from -6 to 6
- value_tangent: bfloat16 [16, 2304, 2048], P('dp', 'seq'), may hold values from -24 to 24
- latents: bfloat16 [16, 2048, 2048], P('dp', 'seq'), may hold values from -3 to 3
- latent_tangent: bfloat16 [16, 2048, 2048], P('dp', 'seq'), may hold values from -3 to 3
- modulation: bfloat16 [16, 2, 2048], P('dp'), may hold values from -2.5 to 2.5
- out_weight: bfloat16 [2048, 2048], P('dp'), may hold values from -0.125 to 0.125
Outputs:
- blended: bfloat16 [16, 2048, 2048], P('dp', 'seq')
- blended_tan: bfloat16 [16, 2048, 2048], P('dp', 'seq')
- weight_grad: float32 [2048, 2048], P('dp', 'seq')
The draws below stay inside these ranges and needn't reach their ends.
All inputs are finite; a program needn't handle non-finite values.
Results may differ from the reference program's by a relative error of at most 0.011.
Values may be sent and summed in bfloat16 or wider, within the bound.
A program may use at most 128 MiB of HBM per device.

```python
import math
import jax
import jax.numpy as jnp
from jax import lax

HEADS = 32
HEAD = 64
FEAT = 2048
INNER = 2048
IMG = 2048
KEYS = 2304
SAMPLES = 16


def shared_rows(key):
    shape = (SAMPLES, KEYS, HEADS * HEAD)
    normal_rows = 1.4 * jax.random.truncated_normal(jax.random.fold_in(key, 11), -4.0, 4.0, shape, jnp.float32)
    return normal_rows


def draw_key_vectors(key, part):
    normal_rows = shared_rows(key)
    return normal_rows.astype(jnp.bfloat16)


def draw_queries(key, part):
    key = jax.random.fold_in(key, 5)
    shape = (SAMPLES, IMG, HEADS * HEAD)
    return (1.4 * jax.random.truncated_normal(key, -4.0, 4.0, shape, jnp.float32)).astype(jnp.bfloat16)


def shard_levels(stream_key, extent, pieces, least, largest):
    def one(dim, shards_of):
        heights = jax.random.uniform(jax.random.fold_in(jax.random.fold_in(stream_key, 6), dim), (shards_of,), jnp.float32, least / len(pieces), largest / len(pieces))
        return jnp.repeat(jnp.exp(heights), extent[dim] // shards_of).reshape((-1,) + (1,) * (len(extent) - dim - 1))

    gain = one(*pieces[0])
    for cut in pieces[1:]:
        gain = gain * one(*cut)
    return gain


def normal_values(stream_key, extent, scale, reach, pieces=(), kind=jnp.bfloat16):
    entries = scale * jax.random.normal(stream_key, extent, jnp.float32)
    if pieces:
        entries = entries * shard_levels(stream_key, extent, pieces, -0.22, 0.18)
    return jnp.clip(entries, -reach, reach).astype(kind)


def setup_inputs(seed: int = 0) -> dict:
    splits = jax.random.split(jax.random.key(seed), 11)
    return {
        "queries": draw_queries(jax.random.fold_in(splits[10], 71), 0),
        "key_vectors": draw_key_vectors(jax.random.fold_in(splits[10], 71), 0),
        "value_vectors": normal_values(splits[2], (SAMPLES, KEYS, INNER), 4.0, 24.0, ((0, 16), (1, 16))),
        "query_tangent": normal_values(splits[3], (SAMPLES, IMG, INNER), 1.0, 6.0, ((0, 16), (1, 16))),
        "key_tangent": normal_values(splits[4], (SAMPLES, KEYS, INNER), 1.0, 6.0, ((0, 16), (1, 16))),
        "value_tangent": normal_values(splits[5], (SAMPLES, KEYS, INNER), 4.0, 24.0, ((0, 16), (1, 16))),
        "latents": normal_values(splits[6], (SAMPLES, IMG, FEAT), 0.5, 3.0, ((0, 16), (1, 16))),
        "latent_tangent": normal_values(splits[7], (SAMPLES, IMG, FEAT), 0.5, 3.0, ((0, 16), (1, 16))),
        "modulation": normal_values(splits[8], (SAMPLES, 2, FEAT), 0.5, 2.5, ((0, 16),)),
        "out_weight": normal_values(splits[9], (INNER, FEAT), INNER ** -0.5, 0.125, ((0, 16),)),
    }


def cross_scores(left, right):
    return lax.dot_general(left, right, (((1,), (1,)), ((), ())), preferred_element_type=jnp.float32)

def attend_block(query_rows, query_tan, key_rows, value_rows, key_tan, value_tan):
    factor = 1.0 / math.sqrt(HEAD)
    scores = cross_scores(query_rows, key_rows) * factor
    score_tan = (cross_scores(query_tan, key_rows) + cross_scores(query_rows, key_tan)) * factor
    row_peak = lax.optimization_barrier(jnp.max(scores, axis=1, keepdims=True))
    shifted = jnp.exp(scores - row_peak)
    softmax = shifted / lax.optimization_barrier(jnp.sum(shifted, axis=1, keepdims=True))
    softmax_low = softmax.astype(jnp.bfloat16)
    combined = jnp.dot(softmax_low, value_rows, preferred_element_type=jnp.float32)
    weighted = softmax * score_tan
    row_total = lax.optimization_barrier(jnp.sum(weighted, axis=1, keepdims=True))
    weighted_low = weighted.astype(jnp.bfloat16)
    combined_tan = jnp.dot(weighted_low, value_rows, preferred_element_type=jnp.float32)
    combined_tan = combined_tan + jnp.dot(softmax_low, value_tan, preferred_element_type=jnp.float32)
    combined_tan = combined_tan - row_total * combined
    return (combined.astype(jnp.bfloat16), combined_tan.astype(jnp.bfloat16))

def split_heads(matrix):
    return matrix.reshape(matrix.shape[0], HEADS, HEAD).transpose(1, 0, 2)

def join_heads(stacked):
    return stacked.transpose(1, 0, 2).reshape(stacked.shape[1], HEADS * HEAD)

def reference(queries, key_vectors, value_vectors, query_tangent, key_tangent, value_tangent, latents, latent_tangent, modulation, out_weight):

    def per_sample(total, items):
        query_s, key_s, value_s, qtan_s, ktan_s, vtan_s, latent_s, ltan_s, gate_s = items
        head_items = (split_heads(query_s), split_heads(qtan_s), split_heads(key_s), split_heads(value_s), split_heads(ktan_s), split_heads(vtan_s))
        head_out, head_tan = lax.map(lambda group: attend_block(*group), head_items)
        attn_out = join_heads(head_out)
        attn_tan = join_heads(head_tan)
        proj = jnp.dot(attn_out, out_weight, preferred_element_type=jnp.float32)
        proj_tan = jnp.dot(attn_tan, out_weight, preferred_element_type=jnp.float32)
        gate = gate_s[0].astype(jnp.float32)
        gate_tan = gate_s[1].astype(jnp.float32)
        blended = (latent_s.astype(jnp.float32) + gate * proj).astype(jnp.bfloat16)
        tangent_f = ltan_s.astype(jnp.float32) + gate_tan * proj + gate * proj_tan
        length = jnp.sqrt(lax.optimization_barrier(jnp.sum(tangent_f * tangent_f, axis=1, keepdims=True)))
        direction = (gate * tangent_f / (length + 0.1)).astype(jnp.bfloat16)
        term = lax.dot_general(attn_out, direction, (((0,), (0,)), ((), ())), preferred_element_type=jnp.float32)
        return (total + term, (blended, tangent_f.astype(jnp.bfloat16)))
    start = jnp.zeros((HEADS * HEAD, FEAT), jnp.float32)
    items = (queries, key_vectors, value_vectors, query_tangent, key_tangent, value_tangent, latents, latent_tangent, modulation)
    total, outputs = lax.scan(per_sample, start, items)
    return (outputs[0], outputs[1], -2.0 * total)
```

```python
import functools
import math

import jax
import jax.numpy as jnp
from jax import lax
from jax.experimental import pallas as pl
from jax.experimental.pallas import tpu as pltpu
from jax.sharding import PartitionSpec as P

MESH = pl.DeviceIdType.MESH
ANY = pl.BlockSpec(memory_space=pl.ANY)
VM = pl.BlockSpec(memory_space=pltpu.VMEM)
GROUP = 16
LANES = 128
HEAD = 64
TOK = 128
KEY_ROWS = 144
TOKENS = GROUP * TOK
KEYS = GROUP * KEY_ROWS
FEAT = 2048
BLOCK = 2 * TOK
TILE = 256
FACTOR = 1.0 / math.sqrt(HEAD)
EXP2_FACTOR = math.log2(math.e) * FACTOR


def dot(left, right):
    return jnp.dot(left, right, preferred_element_type=jnp.float32)


def dot_rows(left, right):
    return lax.dot_general(
        left, right, (((1,), (1,)), ((), ())), preferred_element_type=jnp.float32
    )


def dot_columns(left, right):
    return lax.dot_general(
        left, right, (((0,), (0,)), ((), ())), preferred_element_type=jnp.float32
    )


def lanes_of(index):
    return pl.ds(pl.multiple_of(index * LANES, LANES), LANES)


def rows_of(index, rows):
    return pl.ds(pl.multiple_of(index * rows, 16), rows)


def remote(src, dst, send, recv, device):
    return pltpu.make_async_remote_copy(
        src, dst, send, recv, device_id=device, device_id_type=MESH
    )


def attention_kernel(
    q, k, v, qt, kt, vt,
    ret, heads_out,
    q_in, k_in, v_in, qt_in, kt_in, vt_in,
    keys, values_a, values_b, lhs, scores, heads_tan,
    send, recv, recv_q, local, back_send, back_recv, back_local,
):
    me = lax.axis_index("seq")
    dp = lax.axis_index("dp")
    chip = me // 2
    sibling = jnp.bitwise_xor(me, 1)

    barrier = pltpu.get_barrier_semaphore()

    def greet(step, carry):
        pl.semaphore_signal(
            barrier, 1, device_id=(dp, jnp.bitwise_xor(me, step)), device_id_type=MESH
        )
        return carry

    lax.fori_loop(1, GROUP, greet, 0)
    pl.semaphore_wait(barrier, GROUP - 1)

    keyed = ((k, k_in), (kt, kt_in), (v, v_in), (vt, vt_in))
    queried = ((q, q_in), (qt, qt_in))

    def own(slot, src, dst, rows):
        return pltpu.make_async_copy(
            src.at[0, :, lanes_of(me)], dst.at[rows_of(me, rows), :], local.at[slot]
        )

    for slot, (src, dst) in enumerate(keyed):
        own(slot, src, dst, KEY_ROWS).start()

        def send_keys(step, carry, slot=slot, src=src, dst=dst):
            partner = jnp.bitwise_xor(me, step)
            remote(
                src.at[0, :, lanes_of(partner)], dst.at[rows_of(me, KEY_ROWS), :],
                send.at[slot], recv.at[slot], (dp, partner),
            ).start()
            return carry

        lax.fori_loop(1, GROUP, send_keys, 0)
    for slot, (src, dst) in enumerate(queried):
        own(4 + slot, src, dst, TOK).start()

    def send_queries(step, carry):
        partner = jnp.bitwise_xor(me, step)
        for slot, (src, dst) in enumerate(queried):
            remote(
                src.at[0, :, lanes_of(partner)], dst.at[rows_of(me, TOK), :],
                send.at[4 + slot], recv_q.at[chip], (dp, partner),
            ).start()
        return carry

    lax.fori_loop(1, GROUP, send_queries, 0)

    def all_keys(slot, dst):
        part = dst.at[pl.ds(0, (GROUP - 1) * KEY_ROWS), :]
        return remote(part, part, send.at[slot], recv.at[slot], (dp, sibling))

    lane = lax.broadcasted_iota(jnp.int32, (1, LANES), 1)
    low = lane < HEAD
    one = jnp.ones((), jnp.bfloat16)
    zero = jnp.zeros((), jnp.bfloat16)
    for slot, (src, dst) in enumerate(keyed):
        own(slot, src, dst, KEY_ROWS).wait()
        all_keys(slot, dst).wait_recv()
        if slot == 0:
            keys[:, :LANES] = k_in[...]
        elif slot == 1:
            keys[:, LANES:] = kt_in[...]
        elif slot == 2:
            values = v_in[...]
            values_a[:, :LANES] = jnp.where(low, values, one)
            values_b[:, :LANES] = jnp.where(low, one, values)
        else:
            values = vt_in[...]
            values_a[:, LANES:] = jnp.where(low, values, zero)
            values_b[:, LANES:] = jnp.where(low, zero, values)

    tiles = KEYS // TILE

    def block_scores(rows, head):
        mine = low if head == 0 else jnp.logical_not(low)
        query = jnp.where(mine, q_in[rows, :], zero)
        lhs[head, :BLOCK, :LANES] = query
        lhs[head, :BLOCK, LANES:] = jnp.zeros_like(query)
        lhs[head, BLOCK:, :LANES] = jnp.where(mine, qt_in[rows, :], zero)
        lhs[head, BLOCK:, LANES:] = query
        peak = None
        for tile in range(tiles):
            part = slice(tile * TILE, (tile + 1) * TILE)
            result = dot_rows(lhs[head], keys[part, :])
            scores[head, :, part] = result
            for column in range(TILE // LANES):
                piece = result[:BLOCK, column * LANES : (column + 1) * LANES]
                peak = piece if peak is None else jnp.maximum(peak, piece)
        return peak

    def block_values(head, peak):
        top = jnp.max(peak, axis=1, keepdims=True)
        values = (values_a, values_b)[head]
        total = None
        for tile in range(tiles):
            part = slice(tile * TILE, (tile + 1) * TILE)
            shifted = jnp.exp2((scores[head, :BLOCK, part] - top) * EXP2_FACTOR)
            weighted = shifted * scores[head, BLOCK:, part]
            pair = jnp.concatenate([shifted, weighted], 0).astype(jnp.bfloat16)
            term = dot(pair, values[part, :])
            total = term if total is None else total + term
        plain = total[:BLOCK, :LANES]
        tangent = total[BLOCK:, :LANES]
        inverse = 1.0 / pltpu.roll(plain, HEAD, 1)
        combined = plain * inverse
        row_total = pltpu.roll(tangent, HEAD, 1) * inverse
        combined_tan = (tangent * FACTOR + total[:BLOCK, LANES:]) * inverse
        return combined, combined_tan - FACTOR * row_total * combined

    def hand_back(partner):
        rows = rows_of(partner, TOK)
        pieces = ((heads_out, 0), (heads_tan, TOK))

        @pl.when(partner != me)
        def _():
            for held, place in pieces:
                remote(
                    held.at[rows, :], ret.at[pl.ds(place, TOK), lanes_of(me)],
                    back_send, back_recv, (dp, partner),
                ).start()

        @pl.when(partner == me)
        def _():
            for slot, (held, place) in enumerate(pieces):
                pltpu.make_async_copy(
                    held.at[rows, :], ret.at[pl.ds(place, TOK), lanes_of(me)],
                    back_local.at[slot],
                ).start()

    def body(step, carry):
        other = jnp.bitwise_xor(chip, step)

        @pl.when(step == 0)
        def _():
            for slot, (src, dst) in enumerate(queried):
                own(4 + slot, src, dst, TOK).wait()
            part = q_in.at[pl.ds(0, 2 * TOK), :]
            remote(part, part, send.at[4], recv_q.at[chip], (dp, sibling)).wait_recv()

        @pl.when(step > 0)
        def _():
            part = q_in.at[pl.ds(0, 4 * TOK), :]
            remote(part, part, send.at[4], recv_q.at[other], (dp, sibling)).wait_recv()

        rows = rows_of(other, BLOCK)
        peak_a = block_scores(rows, 0)
        peak_b = block_scores(rows, 1)
        out_a, tan_a = block_values(0, peak_a)
        out_b, tan_b = block_values(1, peak_b)
        heads_out[rows, :] = jnp.where(low, out_a, out_b).astype(jnp.bfloat16)
        heads_tan[rows, :] = jnp.where(low, tan_a, tan_b).astype(jnp.bfloat16)
        for core in range(2):
            hand_back(2 * other + core)
        return carry

    lax.fori_loop(0, GROUP // 2, body, 0)

    for slot, (src, dst) in enumerate(keyed):
        all_keys(slot, dst).wait_send()
    for slot, (src, dst) in enumerate(queried):
        part = dst.at[pl.ds(0, (GROUP - 1) * TOK), :]
        remote(part, part, send.at[4 + slot], recv_q.at[0], (dp, sibling)).wait_send()
    for slot, (held, place) in enumerate(((heads_out, 0), (heads_tan, TOK))):
        pltpu.make_async_copy(
            held.at[rows_of(me, TOK), :], ret.at[pl.ds(place, TOK), lanes_of(me)],
            back_local.at[slot],
        ).wait()
    part = ret.at[pl.ds(0, 2 * TOK * (GROUP - 1) // GROUP), :]
    back = remote(part, part, back_send, back_recv, (dp, sibling))
    back.wait_send()
    back.wait_recv()


def attention(q, k, v, qt, kt, vt):
    half = jnp.bfloat16
    return pl.pallas_call(
        attention_kernel,
        out_shape=[
            jax.ShapeDtypeStruct((2 * TOK, FEAT), half),
            jax.ShapeDtypeStruct((TOKENS, LANES), half),
        ],
        in_specs=[ANY] * 6,
        out_specs=[ANY, VM],
        scratch_shapes=[
            pltpu.VMEM((TOKENS, LANES), half),
            pltpu.VMEM((KEYS, LANES), half),
            pltpu.VMEM((KEYS, LANES), half),
            pltpu.VMEM((TOKENS, LANES), half),
            pltpu.VMEM((KEYS, LANES), half),
            pltpu.VMEM((KEYS, LANES), half),
            pltpu.VMEM((KEYS, 2 * LANES), half),
            pltpu.VMEM((KEYS, 2 * LANES), half),
            pltpu.VMEM((KEYS, 2 * LANES), half),
            pltpu.VMEM((2, 2 * BLOCK, 2 * LANES), half),
            pltpu.VMEM((2, 2 * BLOCK, KEYS), jnp.float32),
            pltpu.VMEM((TOKENS, LANES), half),
            pltpu.SemaphoreType.DMA((6,)),
            pltpu.SemaphoreType.DMA((4,)),
            pltpu.SemaphoreType.DMA((GROUP // 2,)),
            pltpu.SemaphoreType.DMA((6,)),
            pltpu.SemaphoreType.DMA,
            pltpu.SemaphoreType.DMA,
            pltpu.SemaphoreType.DMA((2,)),
        ],
        compiler_params=pltpu.CompilerParams(
            collective_id=0, has_side_effects=True, vmem_limit_bytes=56 * 2**20
        ),
        name="attention",
        cost_estimate=pl.CostEstimate(
            flops=7_250_000_000, bytes_accessed=10_000_000, transcendentals=9_437_184
        ),
    )(q, k, v, qt, kt, vt)


WCHUNK = 256
HALF_HEADS = 8


def output_kernel(
    ret, heads, weight, latents, latent_tan, modulation,
    blended_out, tan_out, grad_out,
    w_in, tangent, proj, direction, heads_in, dir_in, partial, shares,
    w_sem, a_local, a_send, a_recv, f_send, f_recv, d_send, d_recv, d_local,
    g_send, g_recv, g_local,
):
    me = lax.axis_index("seq")
    dp = lax.axis_index("dp")
    x = me // 4
    z = (me // 2) % 2
    core = me % 2
    sibling = jnp.bitwise_xor(me, 1)
    grad_z = (dp // 2) % 2
    grad_from = (me // 4) * 4 + grad_z * 2 + (me % 4) // 2
    grad_self = grad_from == me

    for chunk in range(FEAT // WCHUNK):
        part = pl.ds(chunk * WCHUNK, WCHUNK)
        pltpu.make_async_copy(weight.at[:, part], w_in.at[:, part], w_sem.at[chunk]).start()
    mine = 2 * x + core
    keep = pltpu.make_async_copy(heads, heads_in.at[:, lanes_of(mine)], a_local)
    keep.start()

    barrier = pltpu.get_barrier_semaphore()

    def greet(step, carry):
        pl.semaphore_signal(
            barrier, 1, device_id=(dp, jnp.bitwise_xor(me, step)), device_id_type=MESH
        )
        return carry

    lax.fori_loop(1, GROUP, greet, 0)

    def greet_grad(step, carry):
        @pl.when(jnp.logical_or(step != dp, jnp.logical_not(grad_self)))
        def _():
            pl.semaphore_signal(barrier, 1, device_id=(step, grad_from), device_id_type=MESH)

        return carry

    lax.fori_loop(0, GROUP, greet_grad, 0)
    pl.semaphore_wait(barrier, 2 * GROUP - 1 - grad_self.astype(jnp.int32))

    def spread(step):
        partner = jnp.bitwise_xor(me, 4 * step)
        return remote(
            heads, heads_in.at[:, lanes_of(mine)], a_send.at[step], a_recv.at[step], (dp, partner)
        )

    def forward(step):
        block = 2 * jnp.bitwise_xor(x, step) + core
        held = heads_in.at[:, lanes_of(block)]
        return remote(held, held, f_send.at[step], f_recv.at[step], (dp, sibling))

    for step in (1, 3, 2):
        spread(step).start()
    keep.wait()
    forward(0).start()

    gate = modulation[0, 0:1, :].astype(jnp.float32)
    gate_tan = modulation[0, 1:2, :].astype(jnp.float32)
    square = jnp.zeros((TOK, LANES), jnp.float32)
    for chunk in range(FEAT // WCHUNK):
        part = pl.ds(chunk * WCHUNK, WCHUNK)
        span = slice(chunk * WCHUNK, (chunk + 1) * WCHUNK)
        pltpu.make_async_copy(weight.at[:, part], w_in.at[:, part], w_sem.at[chunk]).wait()
        both = dot(ret[...], w_in[:, span])
        plain = both[:TOK]
        blended_out[0, :, span] = (
            latents[0, :, span].astype(jnp.float32) + gate[:, span] * plain
        ).astype(jnp.bfloat16)
        value = (
            latent_tan[0, :, span].astype(jnp.float32)
            + gate_tan[:, span] * plain
            + gate[:, span] * both[TOK:]
        )
        tangent[:, span] = value
        tan_out[0, :, span] = value.astype(jnp.bfloat16)
        power = value * value
        for column in range(WCHUNK // LANES):
            square = square + power[:, column * LANES : (column + 1) * LANES]
    length = jnp.sqrt(jnp.sum(square, axis=1, keepdims=True))
    scale = 1.0 / (length + 0.1)
    for chunk in range(FEAT // WCHUNK):
        span = slice(chunk * WCHUNK, (chunk + 1) * WCHUNK)
        direction[:, span] = (gate[:, span] * tangent[:, span] * scale).astype(jnp.bfloat16)

    def columns_for(partner):
        return pl.ds(pl.multiple_of((2 * (partner // 4) + partner % 2) * 256, 256), 256)

    def send_direction(step, carry):
        partner = jnp.bitwise_xor(me, step)
        remote(
            direction.at[:, columns_for(partner)], dir_in.at[rows_of(me, TOK), :],
            d_send, d_recv, (dp, partner),
        ).start()
        return carry

    lax.fori_loop(1, GROUP, send_direction, 0)
    own = pltpu.make_async_copy(
        direction.at[:, columns_for(me)], dir_in.at[rows_of(me, TOK), :], d_local
    )
    own.start()

    for step in (1, 3, 2):
        spread(step).wait_recv()
        forward(step).start()
    own.wait()
    part = dir_in.at[pl.ds(0, (GROUP - 1) * TOK), :]
    every = remote(part, part, d_send, d_recv, (dp, sibling))
    every.wait_recv()
    for step in range(4):
        forward(step).wait_recv()
    partial[...] = dot_columns(dir_in[...], heads_in[...]).astype(jnp.bfloat16)

    def share(block, column):
        row = 4 * (block // 2) + 2 * z + block % 2
        place = 4 * x + 2 * core + column
        return row, place, partial.at[pl.ds(column * LANES, LANES), lanes_of(block)]

    def send_shares(step, carry):
        block = jnp.bitwise_xor(step, 2 * x + core)
        for column in range(2):
            row, place, held = share(block, column)
            to_self = jnp.logical_and(row == dp, place == me)

            @pl.when(jnp.logical_not(to_self))
            def _():
                remote(held, shares.at[dp], g_send, g_recv, (row, place)).start()

            @pl.when(to_self)
            def _():
                pltpu.make_async_copy(held, shares.at[dp], g_local).start()

        return carry

    lax.fori_loop(0, HALF_HEADS, send_shares, 0)

    @pl.when(grad_self)
    def _():
        part = shares.at[pl.ds(0, GROUP - 1)]
        pltpu.make_async_copy(shares.at[0], shares.at[1], g_local).wait()
        whole = remote(part, part, g_send, g_recv, (dp, sibling))
        whole.wait_send()
        whole.wait_recv()

    @pl.when(jnp.logical_not(grad_self))
    def _():
        whole = remote(shares, shares, g_send, g_recv, (dp, sibling))
        whole.wait_send()
        whole.wait_recv()

    total = shares[0].astype(jnp.float32)
    for sample in range(1, GROUP):
        total = total + shares[sample].astype(jnp.float32)
    grad_out[...] = -2.0 * total.T

    every.wait_send()
    for step in (1, 3, 2):
        spread(step).wait_send()
    for step in range(4):
        forward(step).wait_send()


def output(ret, heads, weight, latents, latent_tan, modulation):
    half = jnp.bfloat16
    dma = pltpu.SemaphoreType.DMA
    return pl.pallas_call(
        output_kernel,
        out_shape=[
            jax.ShapeDtypeStruct((1, TOK, FEAT), half),
            jax.ShapeDtypeStruct((1, TOK, FEAT), half),
            jax.ShapeDtypeStruct((LANES, LANES), jnp.float32),
        ],
        in_specs=[VM, VM, ANY, VM, VM, VM],
        out_specs=[VM, VM, VM],
        scratch_shapes=[
            pltpu.VMEM((FEAT, FEAT), half),
            pltpu.VMEM((TOK, FEAT), jnp.float32),
            pltpu.VMEM((8, LANES), jnp.float32),
            pltpu.VMEM((TOK, FEAT), half),
            pltpu.VMEM((TOKENS, HALF_HEADS * LANES), half),
            pltpu.VMEM((TOKENS, 256), half),
            pltpu.VMEM((256, HALF_HEADS * LANES), half),
            pltpu.VMEM((GROUP, LANES, LANES), half),
            dma((FEAT // WCHUNK,)),
            dma, dma((4,)), dma((4,)), dma((4,)), dma((4,)), dma, dma, dma,
            dma, dma, dma,
        ],
        compiler_params=pltpu.CompilerParams(
            collective_id=1, has_side_effects=True, vmem_limit_bytes=56 * 2**20
        ),
        name="output",
        cost_estimate=pl.CostEstimate(
            flops=3_300_000_000, bytes_accessed=14_000_000, transcendentals=0
        ),
    )(ret, heads, weight, latents, latent_tan, modulation)


def shards(
    queries, key_vectors, value_vectors, query_tangent, key_tangent, value_tangent,
    latents, latent_tangent, modulation, out_weight,
):
    weight = lax.all_gather(out_weight, "dp", axis=0, tiled=True)
    ret, heads = attention(
        queries, key_vectors, value_vectors, query_tangent, key_tangent, value_tangent
    )
    return tuple(output(ret, heads, weight, latents, latent_tangent, modulation))


def solution(mesh):
    tokens = P("dp", "seq", None)
    in_specs = (tokens,) * 8 + (P("dp", None, None), P("dp", None))
    out_specs = (tokens, tokens, P("dp", "seq"))
    return jax.shard_map(
        shards, mesh=mesh, in_specs=in_specs, out_specs=out_specs, check_vma=False
    )
```

```python
import functools
import math

import jax
import jax.numpy as jnp
from jax import lax
from jax.experimental import pallas as pl
from jax.experimental.pallas import tpu as pltpu
from jax.sharding import PartitionSpec as P

MESH = pl.DeviceIdType.MESH
ANY = pl.BlockSpec(memory_space=pl.ANY)
VM = pl.BlockSpec(memory_space=pltpu.VMEM)
GROUP = 16
LANES = 128
HEAD = 64
TOK = 128
KEY_ROWS = 144
TOKENS = GROUP * TOK
KEYS = GROUP * KEY_ROWS
FEAT = 2048
BLOCK = 2 * TOK
TILE = 256
FACTOR = 1.0 / math.sqrt(HEAD)
EXP2_FACTOR = math.log2(math.e) * FACTOR
WCHUNK = 256
BACK_ROWS = 2 * TOK * (GROUP - 1) // GROUP
COLUMNS = 512
EARLY = 6
QUARTER = FEAT // 4


def dot(left, right):
    return jnp.dot(left, right, preferred_element_type=jnp.float32)


def dot_rows(left, right):
    return lax.dot_general(
        left, right, (((1,), (1,)), ((), ())), preferred_element_type=jnp.float32
    )


def dot_columns(left, right):
    return lax.dot_general(
        left, right, (((0,), (0,)), ((), ())), preferred_element_type=jnp.float32
    )


def lanes_of(index):
    return pl.ds(pl.multiple_of(index * LANES, LANES), LANES)


def rows_of(index, rows):
    return pl.ds(pl.multiple_of(index * rows, 16), rows)


def heads_of(index):
    place = lax.rem(index, 4)
    return 4 * place + lax.rem(place + index // 4, 4)


def remote(src, dst, send, recv, device):
    return pltpu.make_async_remote_copy(
        src, dst, send, recv, device_id=device, device_id_type=MESH
    )


def whole_kernel(
    q, k, v, qt, kt, vt, latents_hbm, latent_tan_hbm, modulation, weight,
    blended_hbm, tan_hbm, grad_out,
    q_in, k_in, v_in, qt_in, kt_in, vt_in,
    keys, values_a, values_b, lhs, scores, heads_out, heads_tan, ret,
    w_in, latents, latent_tan, tangent, direction, heads_in, dir_in, partial, shares,
    send, recv, recv_q, local, back_send, back_recv, back_local,
    w_send, w_recv, w_forward, w_local, l_sem,
    a_local, a_send, a_recv, f_send, f_recv, d_send, d_recv, d_local,
    g_send, g_recv, g_local, crossed, c_send, c_recv,
    blended_out, tan_out, o_sem,
):
    me = lax.axis_index("seq")
    dp = lax.axis_index("dp")
    chip = me // 2
    x = me // 4
    z = (me // 2) % 2
    core = me % 2
    z_hi = dp // 4
    y = dp % 4
    sibling = jnp.bitwise_xor(me, 1)
    z_pair = jnp.bitwise_xor(me, 2)
    next_dp = 4 * lax.rem(z_hi + 2 * z + 3, 4) + y
    grad_from = 4 * lax.rem(y + 4 - z_hi, 4) + me % 4
    grad_self = grad_from == me

    barrier = pltpu.get_barrier_semaphore()

    def greet(step, carry):
        pl.semaphore_signal(
            barrier, 1, device_id=(dp, jnp.bitwise_xor(me, step)), device_id_type=MESH
        )
        return carry

    lax.fori_loop(1, GROUP, greet, 0)

    def greet_row(step, carry):
        pl.semaphore_signal(
            barrier, 1, device_id=(jnp.bitwise_xor(dp, step), me), device_id_type=MESH
        )
        return carry

    lax.fori_loop(1, 4, greet_row, 0)
    pl.semaphore_signal(barrier, 1, device_id=(next_dp, z_pair), device_id_type=MESH)

    keep_weight = pltpu.make_async_copy(weight, w_in.at[rows_of(dp, TOK), :], w_local)
    keep_weight.start()
    load_latents = pltpu.make_async_copy(latents_hbm, latents, l_sem.at[0])
    load_latents.start()
    load_tan = pltpu.make_async_copy(latent_tan_hbm, latent_tan, l_sem.at[1])
    load_tan.start()
    pl.semaphore_wait(barrier, GROUP - 1 + 4)

    half_rows = TOK // 2

    def weight_rows(block):
        return w_in.at[pl.ds(pl.multiple_of(block * TOK + core * half_rows, half_rows), half_rows), :]

    def send_weight(block, device):
        held = weight_rows(block)
        remote(held, held, w_send, w_recv.at[block], device).start()

    def wait_weight(block):
        held = weight_rows(block)
        remote(held, held, w_send, w_recv.at[block], (dp, sibling)).wait_recv()

    def send_weight_rows(block):
        def one(step, carry):
            send_weight(block, (jnp.bitwise_xor(dp, step), me))
            return carry

        lax.fori_loop(1, 4, one, 0)

    def forward_weight(block):
        held = weight_rows(block)
        remote(held, held, w_send, w_forward, (dp, sibling)).start()

    def forward_weight_rows(block):
        def one(step, carry):
            other = jnp.bitwise_xor(block, step)
            wait_weight(other)
            forward_weight(other)
            return carry

        lax.fori_loop(1, 4, one, 0)

    second = next_dp
    third = 4 * lax.rem(z_hi + 2 * (1 - z) + 3, 4) + y
    fourth = 4 * lax.rem(z_hi + 2, 4) + y

    keyed = ((k, k_in), (kt, kt_in), (v, v_in), (vt, vt_in))
    queried = ((q, q_in), (qt, qt_in))

    def own(slot, src, dst, rows):
        return pltpu.make_async_copy(
            src.at[0, :, lanes_of(heads_of(me))], dst.at[rows_of(me, rows), :], local.at[slot]
        )

    keep_weight.wait()
    send_weight(dp, (next_dp, z_pair))
    for slot, (src, dst) in enumerate(keyed):
        own(slot, src, dst, KEY_ROWS).start()

        def send_keys(step, carry, slot=slot, src=src, dst=dst):
            partner = jnp.bitwise_xor(me, step)
            remote(
                src.at[0, :, lanes_of(heads_of(partner))], dst.at[rows_of(me, KEY_ROWS), :],
                send.at[slot], recv.at[slot], (dp, partner),
            ).start()
            return carry

        lax.fori_loop(1, GROUP, send_keys, 0)
        if slot == 1:
            send_weight_rows(dp)
            wait_weight(second)
            send_weight(second, (dp, z_pair))
            send_weight_rows(second)
    for slot, (src, dst) in enumerate(queried):
        own(4 + slot, src, dst, TOK).start()

    def send_queries(step, carry):
        partner = jnp.bitwise_xor(me, step)
        for slot, (src, dst) in enumerate(queried):
            remote(
                src.at[0, :, lanes_of(heads_of(partner))], dst.at[rows_of(me, TOK), :],
                send.at[4 + slot], recv_q.at[chip], (dp, partner),
            ).start()
        return carry

    lax.fori_loop(1, GROUP, send_queries, 0)

    def all_keys(slot, dst):
        part = dst.at[pl.ds(0, (GROUP - 1) * KEY_ROWS), :]
        return remote(part, part, send.at[slot], recv.at[slot], (dp, sibling))

    lane = lax.broadcasted_iota(jnp.int32, (1, LANES), 1)
    low = lane < HEAD
    one = jnp.ones((), jnp.bfloat16)
    zero = jnp.zeros((), jnp.bfloat16)
    for slot, (src, dst) in enumerate(keyed):
        own(slot, src, dst, KEY_ROWS).wait()
        all_keys(slot, dst).wait_recv()
        if slot == 0:
            keys[:, :LANES] = k_in[...]
            forward_weight(second)
            wait_weight(third)
            send_weight(third, (next_dp, z_pair))
            send_weight_rows(third)
            forward_weight(third)
        elif slot == 1:
            keys[:, LANES:] = kt_in[...]
        elif slot == 2:
            values = v_in[...]
            values_a[:, :LANES] = jnp.where(low, values, one)
            values_b[:, :LANES] = jnp.where(low, one, values)
            wait_weight(fourth)
            send_weight_rows(fourth)
            forward_weight(fourth)
        else:
            values = vt_in[...]
            values_a[:, LANES:] = jnp.where(low, values, zero)
            values_b[:, LANES:] = jnp.where(low, zero, values)

    tiles = KEYS // TILE

    def block_scores(rows, head):
        mine = low if head == 0 else jnp.logical_not(low)
        query = jnp.where(mine, q_in[rows, :], zero)
        lhs[head, :BLOCK, :LANES] = query
        lhs[head, :BLOCK, LANES:] = jnp.zeros_like(query)
        lhs[head, BLOCK:, :LANES] = jnp.where(mine, qt_in[rows, :], zero)
        lhs[head, BLOCK:, LANES:] = query
        peak = None
        for tile in range(tiles):
            part = slice(tile * TILE, (tile + 1) * TILE)
            result = dot_rows(lhs[head], keys[part, :])
            scores[head, :, part] = result
            for column in range(TILE // LANES):
                piece = result[:BLOCK, column * LANES : (column + 1) * LANES]
                peak = piece if peak is None else jnp.maximum(peak, piece)
        return peak

    def block_values(head, peak):
        top = jnp.max(peak, axis=1, keepdims=True)
        values = (values_a, values_b)[head]
        total = None
        for tile in range(tiles):
            part = slice(tile * TILE, (tile + 1) * TILE)
            shifted = jnp.exp2((scores[head, :BLOCK, part] - top) * EXP2_FACTOR)
            weighted = shifted * scores[head, BLOCK:, part]
            pair = jnp.concatenate([shifted, weighted], 0).astype(jnp.bfloat16)
            term = dot(pair, values[part, :])
            total = term if total is None else total + term
        plain = total[:BLOCK, :LANES]
        tangent = total[BLOCK:, :LANES]
        inverse = 1.0 / pltpu.roll(plain, HEAD, 1)
        combined = plain * inverse
        row_total = pltpu.roll(tangent, HEAD, 1) * inverse
        combined_tan = (tangent * FACTOR + total[:BLOCK, LANES:]) * inverse
        return combined, combined_tan - FACTOR * row_total * combined

    place = me % 4

    def hand_over(rows):
        remote(
            heads_out.at[rows, :], heads_in.at[rows, lanes_of(place)], a_send, a_recv, (dp, z_pair)
        ).start()

    def hand_back(partner):
        rows = rows_of(partner, TOK)
        pieces = ((heads_out, 0), (heads_tan, TOK))

        @pl.when(partner != me)
        def _():
            for held, first in pieces:
                remote(
                    held.at[rows, :], ret.at[pl.ds(first, TOK), lanes_of(heads_of(me))],
                    back_send, back_recv, (dp, partner),
                ).start()

        @pl.when(partner == me)
        def _():
            for slot, (held, first) in enumerate(pieces):
                pltpu.make_async_copy(
                    held.at[rows, :], ret.at[pl.ds(first, TOK), lanes_of(heads_of(me))],
                    back_local.at[slot],
                ).start()

    def body(step, carry):
        other = jnp.bitwise_xor(chip, step)

        @pl.when(step == 0)
        def _():
            for slot, (src, dst) in enumerate(queried):
                own(4 + slot, src, dst, TOK).wait()
            part = q_in.at[pl.ds(0, 2 * TOK), :]
            remote(part, part, send.at[4], recv_q.at[chip], (dp, sibling)).wait_recv()

        @pl.when(step > 0)
        def _():
            part = q_in.at[pl.ds(0, 4 * TOK), :]
            remote(part, part, send.at[4], recv_q.at[other], (dp, sibling)).wait_recv()

        @pl.when(step == 2)
        def _():
            forward_weight_rows(dp)

        @pl.when(step == 4)
        def _():
            forward_weight_rows(second)

        @pl.when(step == 6)
        def _():
            forward_weight_rows(third)

        rows = rows_of(other, BLOCK)
        peak_a = block_scores(rows, 0)
        peak_b = block_scores(rows, 1)
        out_a, tan_a = block_values(0, peak_a)
        out_b, tan_b = block_values(1, peak_b)
        heads_out[rows, :] = jnp.where(low, out_a, out_b).astype(jnp.bfloat16)
        heads_tan[rows, :] = jnp.where(low, tan_a, tan_b).astype(jnp.bfloat16)
        for side in range(2):
            hand_back(2 * other + side)
        heads_in[rows, lanes_of(place)] = heads_out[rows, :]

        @pl.when(step < EARLY)
        def _():
            hand_over(rows)

        return carry

    lax.fori_loop(0, GROUP // 2, body, 0)

    for slot, (held, first) in enumerate(((heads_out, 0), (heads_tan, TOK))):
        pltpu.make_async_copy(
            held.at[rows_of(me, TOK), :], ret.at[pl.ds(first, TOK), lanes_of(heads_of(me))],
            back_local.at[slot],
        ).wait()


    def hand_rest(step, carry):
        hand_over(rows_of(jnp.bitwise_xor(chip, step), BLOCK))
        return carry

    lax.fori_loop(EARLY, GROUP // 2, hand_rest, 0)
    cross_heads = remote(heads_out, heads_in.at[:, lanes_of(place)], a_send, a_recv, (dp, z_pair))

    def forward(slot, block):
        held = heads_in.at[:, lanes_of(block)]
        return remote(held, held, f_send.at[slot], f_recv.at[slot], (dp, sibling))

    forward(0, place).start()
    forward_weight_rows(fourth)
    part = w_in.at[pl.ds(0, (GROUP - 1) * half_rows), :]
    remote(part, part, w_send, w_forward, (dp, sibling)).wait_recv()
    load_latents.wait()
    load_tan.wait()
    back = remote(
        ret.at[pl.ds(0, BACK_ROWS), :], ret.at[pl.ds(0, BACK_ROWS), :],
        back_send, back_recv, (dp, sibling),
    )
    back.wait_recv()

    gate = modulation[0, 0:1, :].astype(jnp.float32)
    gate_tan = modulation[0, 1:2, :].astype(jnp.float32)
    square = jnp.zeros((TOK, LANES), jnp.float32)
    for chunk in range(FEAT // WCHUNK):
        span = slice(chunk * WCHUNK, (chunk + 1) * WCHUNK)
        both = dot(ret[...], w_in[:, span])
        plain = both[:TOK]
        blended_out[0, :, span] = (
            latents[0, :, span].astype(jnp.float32) + gate[:, span] * plain
        ).astype(jnp.bfloat16)
        value = (
            latent_tan[0, :, span].astype(jnp.float32)
            + gate_tan[:, span] * plain
            + gate[:, span] * both[TOK:]
        )
        tangent[:, span] = value
        tan_out[0, :, span] = value.astype(jnp.bfloat16)
        power = value * value
        for column in range(WCHUNK // LANES):
            square = square + power[:, column * LANES : (column + 1) * LANES]
    store_blended = pltpu.make_async_copy(blended_out, blended_hbm, o_sem.at[0])
    store_blended.start()
    store_tan = pltpu.make_async_copy(tan_out, tan_hbm, o_sem.at[1])
    store_tan.start()
    length = jnp.sqrt(jnp.sum(square, axis=1, keepdims=True))
    scale = 1.0 / (length + 0.1)
    for chunk in range(FEAT // WCHUNK):
        span = slice(chunk * WCHUNK, (chunk + 1) * WCHUNK)
        rounded = (gate[:, span] * tangent[:, span] * scale).astype(jnp.bfloat16)
        for column in range(WCHUNK // LANES):
            block = chunk * (WCHUNK // LANES) + column
            spot = (block % 4) * COLUMNS + (block // 4) * LANES
            direction[:, spot : spot + LANES] = rounded[:, column * LANES : (column + 1) * LANES]

    def piece(group, part):
        return pl.ds(pl.multiple_of(group * COLUMNS, COLUMNS) + part * LANES, LANES)

    def cross(part, side):
        return remote(
            direction.at[:, piece(2 * (1 - z) + side, part)], crossed.at[:, piece(side, part)],
            c_send, c_recv.at[part], (dp, z_pair),
        )

    def cross_wait(part):
        both = crossed.at[:, pl.ds(0, 2 * LANES)]
        return remote(both, both, c_send, c_recv.at[part], (dp, z_pair))

    def spread(part, mine):
        source = me if mine else z_pair

        def one(step, carry):
            partner = jnp.bitwise_xor(me, 4 * (step // 2) + step % 2)
            if mine:
                held = direction.at[:, piece(2 * z + partner % 2, part)]
            else:
                held = crossed.at[:, piece(partner % 2, part)]
            remote(
                held, dir_in.at[rows_of(source, TOK), pl.ds(part * LANES, LANES)],
                d_send, d_recv.at[part], (dp, partner),
            ).start()
            return carry

        lax.fori_loop(1, 8, one, 0)

    def keep_part(part, mine):
        source = me if mine else z_pair
        held = direction.at[:, piece(me % 4, part)] if mine else crossed.at[:, piece(core, part)]
        return pltpu.make_async_copy(
            held, dir_in.at[rows_of(source, TOK), pl.ds(part * LANES, LANES)],
            d_local.at[part, int(mine)],
        )

    def pass_on(part):
        cross_wait(part).wait_recv()
        spread(part, False)
        keep_part(part, False).start()

    for part in range(4):
        for side in range(2):
            cross(part, side).start()
    for part in range(4):
        spread(part, True)
        keep_part(part, True).start()
        if part >= 1:
            pass_on(part - 1)
    pass_on(3)

    cross_heads.wait_recv()
    forward(1, jnp.bitwise_xor(place, 2)).start()
    forward(0, place).wait_recv()
    forward(1, place).wait_recv()

    for part in range(4):
        span = slice(part * LANES, (part + 1) * LANES)
        keep_part(part, True).wait()
        keep_part(part, False).wait()
        every = dir_in.at[pl.ds(0, (GROUP - 2) * TOK), pl.ds(0, LANES)]
        remote(every, every, d_send, d_recv.at[part], (dp, sibling)).wait_recv()
        partial[span, :] = dot_columns(dir_in[:, span], heads_in[...]).astype(jnp.bfloat16)
        owner = 4 * part + me % 4

        def send_shares(step, carry, part=part, owner=owner):
            block = jnp.bitwise_xor(step, z_hi)
            row = heads_of(4 * x + block)
            held = partial.at[pl.ds(part * LANES, LANES), lanes_of(block)]
            to_self = jnp.logical_and(row == dp, owner == me)

            @pl.when(jnp.logical_not(to_self))
            def _():
                remote(held, shares.at[dp], g_send, g_recv, (row, owner)).start()

            @pl.when(to_self)
            def _():
                pltpu.make_async_copy(held, shares.at[dp], g_local).start()

            return carry

        lax.fori_loop(0, 4, send_shares, 0)

    @pl.when(grad_self)
    def _():
        part = shares.at[pl.ds(0, GROUP - 1)]
        pltpu.make_async_copy(shares.at[0], shares.at[1], g_local).wait()
        whole = remote(part, part, g_send, g_recv, (dp, sibling))
        whole.wait_send()
        whole.wait_recv()

    @pl.when(jnp.logical_not(grad_self))
    def _():
        whole = remote(shares, shares, g_send, g_recv, (dp, sibling))
        whole.wait_send()
        whole.wait_recv()

    store_blended.wait()
    store_tan.wait()
    total = shares[0].astype(jnp.float32)
    for sample in range(1, GROUP):
        total = total + shares[sample].astype(jnp.float32)
    grad_out[...] = -2.0 * total.T

    every = dir_in.at[pl.ds(0, (GROUP - 2) * TOK), :]
    remote(every, every, d_send, d_recv.at[0], (dp, sibling)).wait_send()
    remote(crossed, crossed, c_send, c_recv.at[0], (dp, z_pair)).wait_send()
    cross_heads.wait_send()
    forward(0, place).wait_send()
    forward(1, place).wait_send()
    back.wait_send()
    part = w_in.at[pl.ds(0, 2 * (GROUP - 1) * half_rows), :]
    remote(part, part, w_send, w_forward, (dp, sibling)).wait_send()
    for slot, (src, dst) in enumerate(keyed):
        all_keys(slot, dst).wait_send()
    for slot, (src, dst) in enumerate(queried):
        part = dst.at[pl.ds(0, (GROUP - 1) * TOK), :]
        remote(part, part, send.at[4 + slot], recv_q.at[0], (dp, sibling)).wait_send()


def whole(*args):
    half = jnp.bfloat16
    dma = pltpu.SemaphoreType.DMA
    vmem = pltpu.VMEM
    return pl.pallas_call(
        whole_kernel,
        out_shape=[
            jax.ShapeDtypeStruct((1, TOK, FEAT), half),
            jax.ShapeDtypeStruct((1, TOK, FEAT), half),
            jax.ShapeDtypeStruct((LANES, LANES), jnp.float32),
        ],
        in_specs=[ANY] * 8 + [VM, ANY],
        out_specs=[ANY, ANY, VM],
        scratch_shapes=[
            vmem((TOKENS, LANES), half),
            vmem((KEYS, LANES), half),
            vmem((KEYS, LANES), half),
            vmem((TOKENS, LANES), half),
            vmem((KEYS, LANES), half),
            vmem((KEYS, LANES), half),
            vmem((KEYS, 2 * LANES), half),
            vmem((KEYS, 2 * LANES), half),
            vmem((KEYS, 2 * LANES), half),
            vmem((2, 2 * BLOCK, 2 * LANES), half),
            vmem((2, 2 * BLOCK, KEYS), jnp.float32),
            vmem((TOKENS, LANES), half),
            vmem((TOKENS, LANES), half),
            vmem((2 * TOK, FEAT), half),
            vmem((FEAT, FEAT), half),
            vmem((1, TOK, FEAT), half),
            vmem((1, TOK, FEAT), half),
            vmem((TOK, FEAT), jnp.float32),
            vmem((TOK, FEAT), half),
            vmem((TOKENS, QUARTER), half),
            vmem((TOKENS, COLUMNS), half),
            vmem((COLUMNS, QUARTER), half),
            vmem((GROUP, LANES, LANES), half),
            dma((6,)), dma((4,)), dma((GROUP // 2,)), dma((6,)), dma, dma, dma((2,)),
            dma, dma((GROUP,)), dma, dma, dma((2,)),
            dma, dma, dma, dma((2,)), dma((2,)), dma, dma((4,)), dma((4, 2)),
            dma, dma, dma, vmem((TOK, 2 * COLUMNS), half), dma, dma((4,)),
            vmem((1, TOK, FEAT), half), vmem((1, TOK, FEAT), half), dma((2,)),
        ],
        compiler_params=pltpu.CompilerParams(
            collective_id=0, has_side_effects=True, vmem_limit_bytes=56 * 2**20
        ),
        name="whole",
        cost_estimate=pl.CostEstimate(
            flops=10_500_000_000, bytes_accessed=20_000_000, transcendentals=9_437_184
        ),
    )(*args)


def finish_kernel(*refs):
    count = len(refs) // 2
    for index in range(count):
        refs[count + index][...] = refs[index][...]


def finish(arrays):
    return tuple(
        pl.pallas_call(
            finish_kernel,
            out_shape=[jax.ShapeDtypeStruct(array.shape, array.dtype) for array in arrays],
            in_specs=[VM] * len(arrays),
            out_specs=[VM] * len(arrays),
            name="finish",
        )(*arrays)
    )


def shards(
    queries, key_vectors, value_vectors, query_tangent, key_tangent, value_tangent,
    latents, latent_tangent, modulation, out_weight,
):
    return finish(
        whole(
            queries, key_vectors, value_vectors, query_tangent, key_tangent, value_tangent,
            latents, latent_tangent, modulation, out_weight,
        )
    )


def solution(mesh):
    tokens = P("dp", "seq", None)
    in_specs = (tokens,) * 8 + (P("dp", None, None), P("dp", None))
    out_specs = (tokens, tokens, P("dp", "seq"))
    return jax.shard_map(
        shards, mesh=mesh, in_specs=in_specs, out_specs=out_specs, check_vma=False
    )
```

```python
import functools
import math

import jax
import jax.numpy as jnp
from jax import lax
from jax.experimental import pallas as pl
from jax.experimental.pallas import tpu as pltpu
from jax.sharding import PartitionSpec as P

MESH = pl.DeviceIdType.MESH
ANY = pl.BlockSpec(memory_space=pl.ANY)
VM = pl.BlockSpec(memory_space=pltpu.VMEM)
GROUP = 16
LANES = 128
HEAD = 64
TOK = 128
KEY_ROWS = 144
TOKENS = GROUP * TOK
KEYS = GROUP * KEY_ROWS
FEAT = 2048
BLOCK = 2 * TOK
TILE = 256
FACTOR = 1.0 / math.sqrt(HEAD)
EXP2_FACTOR = math.log2(math.e) * FACTOR
WCHUNK = 256
BACK_ROWS = 2 * TOK * (GROUP - 1) // GROUP
HALF_HEADS = 8
SUMS = 4
PARTS = 2
EARLY = 6


def dot(left, right):
    return jnp.dot(left, right, preferred_element_type=jnp.float32)


def dot_rows(left, right):
    return lax.dot_general(
        left, right, (((1,), (1,)), ((), ())), preferred_element_type=jnp.float32
    )


def dot_columns(left, right):
    return lax.dot_general(
        left, right, (((0,), (0,)), ((), ())), preferred_element_type=jnp.float32
    )


def lanes_of(index):
    return pl.ds(pl.multiple_of(index * LANES, LANES), LANES)


def rows_of(index, rows):
    return pl.ds(pl.multiple_of(index * rows, 16), rows)


def heads_of(index):
    row = index // 4
    return 4 * row + lax.rem(2 * (index % 2) + (index // 2) % 2 + row, 4)


def remote(src, dst, send, recv, device):
    return pltpu.make_async_remote_copy(
        src, dst, send, recv, device_id=device, device_id_type=MESH
    )


def whole_kernel(
    q, k, v, qt, kt, vt, latents_hbm, latent_tan_hbm, modulation, weight,
    blended_hbm, tan_hbm, grad_out,
    q_in, k_in, v_in, qt_in, kt_in, vt_in,
    keys, values_a, values_b, lhs, scores, heads_out, heads_tan, ret,
    w_in, latents, latent_tan, tangent, direction, heads_in, dir_in, partial, shares,
    send, recv, recv_q, local, back_send, back_recv, back_local,
    w_send, w_recv, w_forward, w_local, l_sem,
    a_local, a_send, a_recv, f_send, f_recv, d_send, d_recv, d_local,
    g_send, g_recv, g_local,
    blended_out, tan_out, o_sem, stage_in, middle, h_send, h_recv,
):
    me = lax.axis_index("seq")
    dp = lax.axis_index("dp")
    chip = me // 2
    x = me // 4
    z = (me // 2) % 2
    core = me % 2
    z_hi = dp // 4
    y = dp % 4
    sibling = jnp.bitwise_xor(me, 1)
    z_pair = jnp.bitwise_xor(me, 2)
    next_dp = 4 * lax.rem(z_hi + 2 * z + 3, 4) + y
    grad_from = 4 * x + 2 * ((y + z_hi) % 2) + z
    grad_self = grad_from == me

    barrier = pltpu.get_barrier_semaphore()

    def greet(step, carry):
        pl.semaphore_signal(
            barrier, 1, device_id=(dp, jnp.bitwise_xor(me, step)), device_id_type=MESH
        )
        return carry

    lax.fori_loop(1, GROUP, greet, 0)

    def greet_row(step, carry):
        pl.semaphore_signal(
            barrier, 1, device_id=(jnp.bitwise_xor(dp, step), me), device_id_type=MESH
        )
        return carry

    lax.fori_loop(1, 4, greet_row, 0)
    pl.semaphore_signal(barrier, 1, device_id=(next_dp, z_pair), device_id_type=MESH)

    keep_weight = pltpu.make_async_copy(weight, w_in.at[rows_of(dp, TOK), :], w_local)
    keep_weight.start()
    load_latents = pltpu.make_async_copy(latents_hbm, latents, l_sem.at[0])
    load_latents.start()
    load_tan = pltpu.make_async_copy(latent_tan_hbm, latent_tan, l_sem.at[1])
    load_tan.start()
    pl.semaphore_wait(barrier, GROUP - 1 + 4)

    half_rows = TOK // 2

    def weight_rows(block):
        return w_in.at[pl.ds(pl.multiple_of(block * TOK + core * half_rows, half_rows), half_rows), :]

    def send_weight(block, device):
        held = weight_rows(block)
        remote(held, held, w_send, w_recv.at[block], device).start()

    def wait_weight(block):
        held = weight_rows(block)
        remote(held, held, w_send, w_recv.at[block], (dp, sibling)).wait_recv()

    def send_weight_rows(block):
        def one(step, carry):
            send_weight(block, (jnp.bitwise_xor(dp, step), me))
            return carry

        lax.fori_loop(1, 4, one, 0)

    def forward_weight(block):
        held = weight_rows(block)
        remote(held, held, w_send, w_forward, (dp, sibling)).start()

    def forward_weight_rows(block):
        def one(step, carry):
            other = jnp.bitwise_xor(block, step)
            wait_weight(other)
            forward_weight(other)
            return carry

        lax.fori_loop(1, 4, one, 0)

    second = next_dp
    third = 4 * lax.rem(z_hi + 2 * (1 - z) + 3, 4) + y
    fourth = 4 * lax.rem(z_hi + 2, 4) + y

    keyed = ((k, k_in), (kt, kt_in), (v, v_in), (vt, vt_in))
    queried = ((q, q_in), (qt, qt_in))

    def own(slot, src, dst, rows):
        return pltpu.make_async_copy(
            src.at[0, :, lanes_of(heads_of(me))], dst.at[rows_of(me, rows), :], local.at[slot]
        )

    keep_weight.wait()
    send_weight(dp, (next_dp, z_pair))
    def all_keys(slot, dst):
        part = dst.at[pl.ds(0, (GROUP - 1) * KEY_ROWS), :]
        return remote(part, part, send.at[slot], recv.at[slot], (dp, sibling))

    for slot, (src, dst) in enumerate(keyed):
        own(slot, src, dst, KEY_ROWS).start()
        if slot >= 2:
            all_keys(slot - 2, keyed[slot - 2][1]).wait_send()

        def send_keys(step, carry, slot=slot, src=src, dst=dst):
            partner = jnp.bitwise_xor(me, step)
            remote(
                src.at[0, :, lanes_of(heads_of(partner))], dst.at[rows_of(me, KEY_ROWS), :],
                send.at[slot], recv.at[slot], (dp, partner),
            ).start()
            return carry

        lax.fori_loop(1, GROUP, send_keys, 0)
        if slot == 1:
            send_weight_rows(dp)
            wait_weight(second)
            send_weight(second, (dp, z_pair))
            send_weight_rows(second)
    for slot, (src, dst) in enumerate(queried):
        own(4 + slot, src, dst, TOK).start()

    all_keys(2, v_in).wait_send()

    def send_queries(step, carry):
        partner = jnp.bitwise_xor(me, step)
        for slot, (src, dst) in enumerate(queried):
            remote(
                src.at[0, :, lanes_of(heads_of(partner))], dst.at[rows_of(me, TOK), :],
                send.at[4 + slot], recv_q.at[chip], (dp, partner),
            ).start()
        return carry

    lax.fori_loop(1, GROUP, send_queries, 0)

    lane = lax.broadcasted_iota(jnp.int32, (1, LANES), 1)
    low = lane < HEAD
    one = jnp.ones((), jnp.bfloat16)
    zero = jnp.zeros((), jnp.bfloat16)
    for slot, (src, dst) in enumerate(keyed):
        own(slot, src, dst, KEY_ROWS).wait()
        all_keys(slot, dst).wait_recv()
        if slot == 0:
            keys[:, :LANES] = k_in[...]
            forward_weight(second)
            wait_weight(third)
            send_weight(third, (next_dp, z_pair))
            send_weight_rows(third)
            forward_weight(third)
        elif slot == 1:
            keys[:, LANES:] = kt_in[...]
        elif slot == 2:
            values = v_in[...]
            values_a[:, :LANES] = jnp.where(low, values, one)
            values_b[:, :LANES] = jnp.where(low, one, values)
            wait_weight(fourth)
            send_weight_rows(fourth)
            forward_weight(fourth)
        else:
            values = vt_in[...]
            values_a[:, LANES:] = jnp.where(low, values, zero)
            values_b[:, LANES:] = jnp.where(low, zero, values)

    tiles = KEYS // TILE

    def block_scores(rows, head):
        mine = low if head == 0 else jnp.logical_not(low)
        query = jnp.where(mine, q_in[rows, :], zero)
        lhs[head, :BLOCK, :LANES] = query
        lhs[head, :BLOCK, LANES:] = jnp.zeros_like(query)
        lhs[head, BLOCK:, :LANES] = jnp.where(mine, qt_in[rows, :], zero)
        lhs[head, BLOCK:, LANES:] = query
        peak = None
        for tile in range(tiles):
            part = slice(tile * TILE, (tile + 1) * TILE)
            result = dot_rows(lhs[head], keys[part, :])
            scores[head, :, part] = result
            for column in range(TILE // LANES):
                piece = result[:BLOCK, column * LANES : (column + 1) * LANES]
                peak = piece if peak is None else jnp.maximum(peak, piece)
        return peak

    def block_values(head, peak):
        top = jnp.max(peak, axis=1, keepdims=True)
        values = (values_a, values_b)[head]
        total = None
        for tile in range(tiles):
            part = slice(tile * TILE, (tile + 1) * TILE)
            shifted = jnp.exp2((scores[head, :BLOCK, part] - top) * EXP2_FACTOR)
            weighted = shifted * scores[head, BLOCK:, part]
            pair = jnp.concatenate([shifted, weighted], 0).astype(jnp.bfloat16)
            term = dot(pair, values[part, :])
            total = term if total is None else total + term
        plain = total[:BLOCK, :LANES]
        tangent = total[BLOCK:, :LANES]
        inverse = 1.0 / pltpu.roll(plain, HEAD, 1)
        combined = plain * inverse
        row_total = pltpu.roll(tangent, HEAD, 1) * inverse
        combined_tan = (tangent * FACTOR + total[:BLOCK, LANES:]) * inverse
        return combined, combined_tan - FACTOR * row_total * combined

    place = 2 * x + core

    def hand_over(rows):
        for step in (2, 1, 3):
            remote(
                heads_out.at[rows, :], heads_in.at[rows, lanes_of(place)],
                a_send.at[step], a_recv.at[step], (dp, jnp.bitwise_xor(me, 4 * step)),
            ).start()

    def hand_back(partner):
        rows = rows_of(partner, TOK)
        pieces = ((heads_out, 0), (heads_tan, TOK))

        @pl.when(partner != me)
        def _():
            for held, first in pieces:
                remote(
                    held.at[rows, :], ret.at[pl.ds(first, TOK), lanes_of(heads_of(me))],
                    back_send, back_recv, (dp, partner),
                ).start()

        @pl.when(partner == me)
        def _():
            for slot, (held, first) in enumerate(pieces):
                pltpu.make_async_copy(
                    held.at[rows, :], ret.at[pl.ds(first, TOK), lanes_of(heads_of(me))],
                    back_local.at[slot],
                ).start()

    def body(step, carry):
        other = jnp.bitwise_xor(chip, step)

        @pl.when(step == 0)
        def _():
            for slot, (src, dst) in enumerate(queried):
                own(4 + slot, src, dst, TOK).wait()
            part = q_in.at[pl.ds(0, 2 * TOK), :]
            remote(part, part, send.at[4], recv_q.at[chip], (dp, sibling)).wait_recv()

        @pl.when(step > 0)
        def _():
            part = q_in.at[pl.ds(0, 4 * TOK), :]
            remote(part, part, send.at[4], recv_q.at[other], (dp, sibling)).wait_recv()

        @pl.when(step == 2)
        def _():
            forward_weight_rows(dp)

        @pl.when(step == 4)
        def _():
            forward_weight_rows(second)

        @pl.when(step == 6)
        def _():
            forward_weight_rows(third)

        rows = rows_of(other, BLOCK)
        peak_a = block_scores(rows, 0)
        peak_b = block_scores(rows, 1)
        out_a, tan_a = block_values(0, peak_a)
        out_b, tan_b = block_values(1, peak_b)
        heads_out[rows, :] = jnp.where(low, out_a, out_b).astype(jnp.bfloat16)
        heads_tan[rows, :] = jnp.where(low, tan_a, tan_b).astype(jnp.bfloat16)
        for side in range(2):
            hand_back(2 * other + side)
        heads_in[rows, lanes_of(place)] = heads_out[rows, :]

        @pl.when(step < EARLY)
        def _():
            hand_over(rows)

        return carry

    lax.fori_loop(0, GROUP // 2, body, 0)

    for slot, (held, first) in enumerate(((heads_out, 0), (heads_tan, TOK))):
        pltpu.make_async_copy(
            held.at[rows_of(me, TOK), :], ret.at[pl.ds(first, TOK), lanes_of(heads_of(me))],
            back_local.at[slot],
        ).wait()


    def hand_rest(step, carry):
        hand_over(rows_of(jnp.bitwise_xor(chip, step), BLOCK))
        return carry

    lax.fori_loop(EARLY, GROUP // 2, hand_rest, 0)
    def handed(step):
        return remote(
            heads_out, heads_in.at[:, lanes_of(place)], a_send.at[step], a_recv.at[step],
            (dp, jnp.bitwise_xor(me, 4 * step)),
        )

    def forward(step):
        held = heads_in.at[:, lanes_of(2 * jnp.bitwise_xor(x, step) + core)]
        return remote(held, held, f_send.at[step], f_recv.at[step], (dp, sibling))

    forward(0).start()
    forward_weight_rows(fourth)
    part = w_in.at[pl.ds(0, (GROUP - 1) * half_rows), :]
    remote(part, part, w_send, w_forward, (dp, sibling)).wait_recv()
    load_latents.wait()
    load_tan.wait()
    back = remote(
        ret.at[pl.ds(0, BACK_ROWS), :], ret.at[pl.ds(0, BACK_ROWS), :],
        back_send, back_recv, (dp, sibling),
    )
    back.wait_recv()

    gate = modulation[0, 0:1, :].astype(jnp.float32)
    gate_tan = modulation[0, 1:2, :].astype(jnp.float32)
    square = jnp.zeros((TOK, LANES), jnp.float32)
    for chunk in range(FEAT // WCHUNK):
        span = slice(chunk * WCHUNK, (chunk + 1) * WCHUNK)
        both = dot(ret[...], w_in[:, span])
        plain = both[:TOK]
        blended_out[0, :, span] = (
            latents[0, :, span].astype(jnp.float32) + gate[:, span] * plain
        ).astype(jnp.bfloat16)
        value = (
            latent_tan[0, :, span].astype(jnp.float32)
            + gate_tan[:, span] * plain
            + gate[:, span] * both[TOK:]
        )
        tangent[:, span] = value
        tan_out[0, :, span] = value.astype(jnp.bfloat16)
        power = value * value
        for column in range(WCHUNK // LANES):
            square = square + power[:, column * LANES : (column + 1) * LANES]
    store_blended = pltpu.make_async_copy(blended_out, blended_hbm, o_sem.at[0])
    store_blended.start()
    store_tan = pltpu.make_async_copy(tan_out, tan_hbm, o_sem.at[1])
    store_tan.start()
    length = jnp.sqrt(jnp.sum(square, axis=1, keepdims=True))
    scale = 1.0 / (length + 0.1)
    for chunk in range(FEAT // WCHUNK):
        span = slice(chunk * WCHUNK, (chunk + 1) * WCHUNK)
        rounded = (gate[:, span] * tangent[:, span] * scale).astype(jnp.bfloat16)
        direction[:, span] = rounded

    def turn(part):
        return (part + z_hi) % 2

    def send_direction(part):
        def one(step, carry):
            partner = jnp.bitwise_xor(me, step)
            remote(
                direction.at[:, lanes_of(4 * (partner // 4) + 2 * (partner % 2) + turn(part))],
                dir_in.at[rows_of(me, TOK), pl.ds(part * LANES, LANES)],
                d_send, d_recv.at[part], (dp, partner),
            ).start()
            return carry

        lax.fori_loop(1, GROUP, one, 0)
        keep_part(part).start()

    def keep_part(part):
        return pltpu.make_async_copy(
            direction.at[:, lanes_of(4 * x + 2 * core + turn(part))],
            dir_in.at[rows_of(me, TOK), pl.ds(part * LANES, LANES)],
            d_local.at[part],
        )

    def finish_part(part):
        span = slice(part * LANES, (part + 1) * LANES)
        keep_part(part).wait()
        others = dir_in.at[pl.ds(0, (GROUP - 1) * TOK), pl.ds(0, LANES)]
        remote(others, others, d_send, d_recv.at[part], (dp, sibling)).wait_recv()
        partial[span, :] = dot_columns(dir_in[:, span], heads_in[...]).astype(jnp.bfloat16)

        def send_rows(step, carry):
            other = jnp.bitwise_xor(y, step)
            for side in range(2):
                remote(
                    partial.at[pl.ds(part * LANES, LANES), lanes_of(block_of(other, side))],
                    stage_in.at[part, step - 1, side], h_send, h_recv.at[part],
                    (jnp.bitwise_xor(dp, step), me),
                ).start()
            return carry

        lax.fori_loop(1, 4, send_rows, 0)

    def block_of(row, side):
        return 2 * lax.rem(row + 8 - z - 2 * side, 4) + side

    def reduce_part(part):
        held = stage_in.at[part]
        remote(held, held, h_send, h_recv.at[part], (dp, sibling)).wait_recv()
        owner = 4 * x + 2 * core + turn(part)
        for side in range(2):
            block = block_of(y, side)
            total = partial[part * LANES : (part + 1) * LANES, lanes_of(block)].astype(jnp.float32)
            for step in range(3):
                total = total + stage_in[part, step, side].astype(jnp.float32)
            middle[part, side] = total.astype(jnp.bfloat16)
            row = 4 * (block // 2) + y
            to_self = jnp.logical_and(row == dp, owner == me)

            @pl.when(jnp.logical_not(to_self))
            def _():
                remote(
                    middle.at[part, side], shares.at[z_hi], g_send, g_recv, (row, owner)
                ).start()

            @pl.when(to_self)
            def _():
                pltpu.make_async_copy(middle.at[part, side], shares.at[z_hi], g_local).start()

    for part in range(PARTS):
        send_direction(part)
    for step in (1, 3, 2):
        handed(step).wait_recv()
        forward(step).start()
    for step in range(4):
        forward(step).wait_recv()
    for part in range(PARTS):
        finish_part(part)
    for part in range(PARTS):
        reduce_part(part)

    @pl.when(grad_self)
    def _():
        part = shares.at[pl.ds(0, SUMS - 1)]
        pltpu.make_async_copy(shares.at[0], shares.at[1], g_local).wait()
        whole = remote(part, part, g_send, g_recv, (dp, sibling))
        whole.wait_send()
        whole.wait_recv()

    @pl.when(jnp.logical_not(grad_self))
    def _():
        whole = remote(shares, shares, g_send, g_recv, (dp, sibling))
        whole.wait_send()
        whole.wait_recv()

    store_blended.wait()
    store_tan.wait()
    total = shares[0].astype(jnp.float32)
    for sample in range(1, SUMS):
        total = total + shares[sample].astype(jnp.float32)
    grad_out[...] = -2.0 * total.T

    remote(stage_in, stage_in, h_send, h_recv.at[0], (dp, sibling)).wait_send()
    others = dir_in.at[pl.ds(0, (GROUP - 1) * TOK), :]
    remote(others, others, d_send, d_recv.at[0], (dp, sibling)).wait_send()
    for step in (1, 3, 2):
        handed(step).wait_send()
    for step in range(4):
        forward(step).wait_send()
    back.wait_send()
    part = w_in.at[pl.ds(0, 2 * (GROUP - 1) * half_rows), :]
    remote(part, part, w_send, w_forward, (dp, sibling)).wait_send()
    all_keys(3, vt_in).wait_send()
    for slot, (src, dst) in enumerate(queried):
        part = dst.at[pl.ds(0, (GROUP - 1) * TOK), :]
        remote(part, part, send.at[4 + slot], recv_q.at[0], (dp, sibling)).wait_send()


def whole(*args):
    half = jnp.bfloat16
    dma = pltpu.SemaphoreType.DMA
    vmem = pltpu.VMEM
    return pl.pallas_call(
        whole_kernel,
        out_shape=[
            jax.ShapeDtypeStruct((1, TOK, FEAT), half),
            jax.ShapeDtypeStruct((1, TOK, FEAT), half),
            jax.ShapeDtypeStruct((LANES, LANES), jnp.float32),
        ],
        in_specs=[ANY] * 8 + [VM, ANY],
        out_specs=[ANY, ANY, VM],
        scratch_shapes=[
            vmem((TOKENS, LANES), half),
            vmem((KEYS, LANES), half),
            vmem((KEYS, LANES), half),
            vmem((TOKENS, LANES), half),
            vmem((KEYS, LANES), half),
            vmem((KEYS, LANES), half),
            vmem((KEYS, 2 * LANES), half),
            vmem((KEYS, 2 * LANES), half),
            vmem((KEYS, 2 * LANES), half),
            vmem((2, 2 * BLOCK, 2 * LANES), half),
            vmem((2, 2 * BLOCK, KEYS), jnp.float32),
            vmem((TOKENS, LANES), half),
            vmem((TOKENS, LANES), half),
            vmem((2 * TOK, FEAT), half),
            vmem((FEAT, FEAT), half),
            vmem((1, TOK, FEAT), half),
            vmem((1, TOK, FEAT), half),
            vmem((TOK, FEAT), jnp.float32),
            vmem((TOK, FEAT), half),
            vmem((TOKENS, HALF_HEADS * LANES), half),
            vmem((TOKENS, PARTS * LANES), half),
            vmem((PARTS * LANES, HALF_HEADS * LANES), half),
            vmem((SUMS, LANES, LANES), half),
            dma((6,)), dma((4,)), dma((GROUP // 2,)), dma((6,)), dma, dma, dma((2,)),
            dma, dma((GROUP,)), dma, dma, dma((2,)),
            dma, dma((4,)), dma((4,)), dma((4,)), dma((4,)), dma, dma((PARTS,)), dma((PARTS,)),
            dma, dma, dma,
            vmem((1, TOK, FEAT), half), vmem((1, TOK, FEAT), half), dma((2,)),
            vmem((PARTS, 3, 2, LANES, LANES), half), vmem((PARTS, 2, LANES, LANES), half),
            dma, dma((PARTS,)),
        ],
        compiler_params=pltpu.CompilerParams(
            collective_id=0, has_side_effects=True, vmem_limit_bytes=56 * 2**20
        ),
        name="whole",
        cost_estimate=pl.CostEstimate(
            flops=10_500_000_000, bytes_accessed=20_000_000, transcendentals=9_437_184
        ),
    )(*args)


def finish_kernel(*refs):
    count = len(refs) // 2
    for index in range(count):
        refs[count + index][...] = refs[index][...]


def finish(arrays):
    return tuple(
        pl.pallas_call(
            finish_kernel,
            out_shape=[jax.ShapeDtypeStruct(array.shape, array.dtype) for array in arrays],
            in_specs=[VM] * len(arrays),
            out_specs=[VM] * len(arrays),
            name="finish",
        )(*arrays)
    )


def shards(
    queries, key_vectors, value_vectors, query_tangent, key_tangent, value_tangent,
    latents, latent_tangent, modulation, out_weight,
):
    return finish(
        whole(
            queries, key_vectors, value_vectors, query_tangent, key_tangent, value_tangent,
            latents, latent_tangent, modulation, out_weight,
        )
    )


def solution(mesh):
    tokens = P("dp", "seq", None)
    in_specs = (tokens,) * 8 + (P("dp", None, None), P("dp", None))
    out_specs = (tokens, tokens, P("dp", "seq"))
    return jax.shard_map(
        shards, mesh=mesh, in_specs=in_specs, out_specs=out_specs, check_vma=False
    )
```

```python
import functools
import math

import jax
import jax.numpy as jnp
from jax import lax
from jax.experimental import pallas as pl
from jax.experimental.pallas import tpu as pltpu
from jax.sharding import PartitionSpec as P

MESH = pl.DeviceIdType.MESH
ANY = pl.BlockSpec(memory_space=pl.ANY)
VM = pl.BlockSpec(memory_space=pltpu.VMEM)
GROUP = 16
LANES = 128
HEAD = 64
TOK = 128
KEY_ROWS = 144
TOKENS = GROUP * TOK
KEYS = GROUP * KEY_ROWS
FEAT = 2048
BLOCK = 2 * TOK
TILE = 256
FACTOR = 1.0 / math.sqrt(HEAD)
EXP2_FACTOR = math.log2(math.e) * FACTOR
WCHUNK = 256
BACK_ROWS = 2 * TOK * (GROUP - 1) // GROUP
HALF_HEADS = 8
SUMS = 4
PARTS = 2
EARLY = 6


def dot(left, right):
    return jnp.dot(left, right, preferred_element_type=jnp.float32)


def dot_rows(left, right):
    return lax.dot_general(
        left, right, (((1,), (1,)), ((), ())), preferred_element_type=jnp.float32
    )


def dot_columns(left, right):
    return lax.dot_general(
        left, right, (((0,), (0,)), ((), ())), preferred_element_type=jnp.float32
    )


def lanes_of(index):
    return pl.ds(pl.multiple_of(index * LANES, LANES), LANES)


def rows_of(index, rows):
    return pl.ds(pl.multiple_of(index * rows, 16), rows)


def heads_of(index):
    row = index // 4
    return 4 * row + lax.rem(2 * (index % 2) + (index // 2) % 2 + row, 4)


def remote(src, dst, send, recv, device):
    return pltpu.make_async_remote_copy(
        src, dst, send, recv, device_id=device, device_id_type=MESH
    )


def whole_kernel(
    q, k, v, qt, kt, vt, latents_hbm, latent_tan_hbm, modulation, weight,
    blended_hbm, tan_hbm, grad_out,
    q_in, k_in, v_in, qt_in, kt_in, vt_in,
    keys, values_a, values_b, lhs, scores, heads_out, heads_tan, ret,
    w_in, latents, latent_tan, tangent, direction, heads_in, dir_in, partial, shares,
    send, recv, recv_q, local, back_send, back_recv, back_local,
    w_send, w_recv, w_forward, w_local, l_sem,
    a_local, a_send, a_recv, f_send, f_recv, d_send, d_recv, d_local,
    g_send, g_recv, g_local,
    blended_out, tan_out, o_sem, stage_in, middle, h_send, h_recv,
):
    me = lax.axis_index("seq")
    dp = lax.axis_index("dp")
    chip = me // 2
    x = me // 4
    z = (me // 2) % 2
    core = me % 2
    z_hi = dp // 4
    y = dp % 4
    sibling = jnp.bitwise_xor(me, 1)
    z_pair = jnp.bitwise_xor(me, 2)
    next_dp = 4 * lax.rem(z_hi + 2 * z + 3, 4) + y
    grad_from = 4 * x + 2 * ((y + z_hi) % 2) + z
    grad_self = grad_from == me

    barrier = pltpu.get_barrier_semaphore()

    def greet(step, carry):
        pl.semaphore_signal(
            barrier, 1, device_id=(dp, jnp.bitwise_xor(me, step)), device_id_type=MESH
        )
        return carry

    lax.fori_loop(1, GROUP, greet, 0)

    def greet_row(step, carry):
        pl.semaphore_signal(
            barrier, 1, device_id=(jnp.bitwise_xor(dp, step), me), device_id_type=MESH
        )
        return carry

    lax.fori_loop(1, 4, greet_row, 0)
    pl.semaphore_signal(barrier, 1, device_id=(next_dp, z_pair), device_id_type=MESH)

    keep_weight = pltpu.make_async_copy(weight, w_in.at[rows_of(dp, TOK), :], w_local)
    keep_weight.start()
    load_latents = pltpu.make_async_copy(latents_hbm, latents, l_sem.at[0])
    load_latents.start()
    load_tan = pltpu.make_async_copy(latent_tan_hbm, latent_tan, l_sem.at[1])
    load_tan.start()
    pl.semaphore_wait(barrier, GROUP - 1 + 4)

    half_rows = TOK // 2

    def weight_rows(block):
        return w_in.at[pl.ds(pl.multiple_of(block * TOK + core * half_rows, half_rows), half_rows), :]

    def send_weight(block, device):
        held = weight_rows(block)
        remote(held, held, w_send, w_recv.at[block], device).start()

    def wait_weight(block):
        held = weight_rows(block)
        remote(held, held, w_send, w_recv.at[block], (dp, sibling)).wait_recv()

    def send_weight_rows(block):
        def one(step, carry):
            send_weight(block, (jnp.bitwise_xor(dp, step), me))
            return carry

        lax.fori_loop(1, 4, one, 0)

    def forward_weight(block):
        held = weight_rows(block)
        remote(held, held, w_send, w_forward, (dp, sibling)).start()

    def forward_weight_rows(block):
        def one(step, carry):
            other = jnp.bitwise_xor(block, step)
            wait_weight(other)
            forward_weight(other)
            return carry

        lax.fori_loop(1, 4, one, 0)

    second = next_dp
    third = 4 * lax.rem(z_hi + 2 * (1 - z) + 3, 4) + y
    fourth = 4 * lax.rem(z_hi + 2, 4) + y

    keyed = ((k, k_in), (kt, kt_in), (v, v_in), (vt, vt_in))
    queried = ((q, q_in), (qt, qt_in))

    def own(slot, src, dst, rows):
        return pltpu.make_async_copy(
            src.at[0, :, lanes_of(heads_of(me))], dst.at[rows_of(me, rows), :], local.at[slot]
        )

    keep_weight.wait()
    send_weight(dp, (next_dp, z_pair))
    def all_keys(slot, dst):
        part = dst.at[pl.ds(0, (GROUP - 1) * KEY_ROWS), :]
        return remote(part, part, send.at[slot], recv.at[slot], (dp, sibling))

    def send_queries(step, carry):
        partner = jnp.bitwise_xor(me, step)
        for slot, (src, dst) in enumerate(queried):
            remote(
                src.at[0, :, lanes_of(heads_of(partner))], dst.at[rows_of(me, TOK), :],
                send.at[4 + slot], recv_q.at[chip], (dp, partner),
            ).start()
        return carry

    for slot, (src, dst) in enumerate(queried):
        own(4 + slot, src, dst, TOK).start()
    send_queries(1, 0)
    for slot, (src, dst) in enumerate(keyed):
        own(slot, src, dst, KEY_ROWS).start()
        if slot >= 2:
            all_keys(slot - 2, keyed[slot - 2][1]).wait_send()

        def send_keys(step, carry, slot=slot, src=src, dst=dst):
            partner = jnp.bitwise_xor(me, step)
            remote(
                src.at[0, :, lanes_of(heads_of(partner))], dst.at[rows_of(me, KEY_ROWS), :],
                send.at[slot], recv.at[slot], (dp, partner),
            ).start()
            return carry

        lax.fori_loop(1, GROUP, send_keys, 0)
        if slot == 1:
            send_weight_rows(dp)
            wait_weight(second)
            send_weight(second, (dp, z_pair))
            send_weight_rows(second)

    all_keys(2, v_in).wait_send()
    lax.fori_loop(2, GROUP, send_queries, 0)

    lane = lax.broadcasted_iota(jnp.int32, (1, LANES), 1)
    low = lane < HEAD
    one = jnp.ones((), jnp.bfloat16)
    zero = jnp.zeros((), jnp.bfloat16)
    tiles = KEYS // TILE

    def block_scores(rows, head):
        mine = low if head == 0 else jnp.logical_not(low)
        query = jnp.where(mine, q_in[rows, :], zero)
        lhs[head, :BLOCK, :LANES] = query
        lhs[head, :BLOCK, LANES:] = jnp.zeros_like(query)
        lhs[head, BLOCK:, :LANES] = jnp.where(mine, qt_in[rows, :], zero)
        lhs[head, BLOCK:, LANES:] = query
        peak = None
        for tile in range(tiles):
            part = slice(tile * TILE, (tile + 1) * TILE)
            result = dot_rows(lhs[head], keys[part, :])
            scores[head, :, part] = result
            for column in range(TILE // LANES):
                piece = result[:BLOCK, column * LANES : (column + 1) * LANES]
                peak = piece if peak is None else jnp.maximum(peak, piece)
        return peak

    for slot, (src, dst) in enumerate(keyed):
        own(slot, src, dst, KEY_ROWS).wait()
        all_keys(slot, dst).wait_recv()
        if slot == 0:
            keys[:, :LANES] = k_in[...]
            forward_weight(second)
            wait_weight(third)
            send_weight(third, (next_dp, z_pair))
            send_weight_rows(third)
            forward_weight(third)
        elif slot == 1:
            keys[:, LANES:] = kt_in[...]
            for kind, (query_src, query_dst) in enumerate(queried):
                own(4 + kind, query_src, query_dst, TOK).wait()
            part = q_in.at[pl.ds(0, 2 * TOK), :]
            remote(part, part, send.at[4], recv_q.at[chip], (dp, sibling)).wait_recv()
            first_peaks = [block_scores(rows_of(chip, BLOCK), head) for head in range(2)]
        elif slot == 2:
            values = v_in[...]
            values_a[:, :LANES] = jnp.where(low, values, one)
            values_b[:, :LANES] = jnp.where(low, one, values)
            wait_weight(fourth)
            send_weight_rows(fourth)
            forward_weight(fourth)
        else:
            values = vt_in[...]
            values_a[:, LANES:] = jnp.where(low, values, zero)
            values_b[:, LANES:] = jnp.where(low, zero, values)

    def block_values(head, peak):
        top = jnp.max(peak, axis=1, keepdims=True)
        values = (values_a, values_b)[head]
        total = None
        for tile in range(tiles):
            part = slice(tile * TILE, (tile + 1) * TILE)
            shifted = jnp.exp2((scores[head, :BLOCK, part] - top) * EXP2_FACTOR)
            weighted = shifted * scores[head, BLOCK:, part]
            pair = jnp.concatenate([shifted, weighted], 0).astype(jnp.bfloat16)
            term = dot(pair, values[part, :])
            total = term if total is None else total + term
        plain = total[:BLOCK, :LANES]
        tangent = total[BLOCK:, :LANES]
        inverse = 1.0 / pltpu.roll(plain, HEAD, 1)
        combined = plain * inverse
        row_total = pltpu.roll(tangent, HEAD, 1) * inverse
        combined_tan = (tangent * FACTOR + total[:BLOCK, LANES:]) * inverse
        return combined, combined_tan - FACTOR * row_total * combined

    place = 2 * x + core

    def hand_over(rows):
        for step in (2, 1, 3):
            remote(
                heads_out.at[rows, :], heads_in.at[rows, lanes_of(place)],
                a_send.at[step], a_recv.at[step], (dp, jnp.bitwise_xor(me, 4 * step)),
            ).start()

    def hand_back(partner):
        rows = rows_of(partner, TOK)
        pieces = ((heads_out, 0), (heads_tan, TOK))

        @pl.when(partner != me)
        def _():
            for held, first in pieces:
                remote(
                    held.at[rows, :], ret.at[pl.ds(first, TOK), lanes_of(heads_of(me))],
                    back_send, back_recv, (dp, partner),
                ).start()

        @pl.when(partner == me)
        def _():
            for slot, (held, first) in enumerate(pieces):
                pltpu.make_async_copy(
                    held.at[rows, :], ret.at[pl.ds(first, TOK), lanes_of(heads_of(me))],
                    back_local.at[slot],
                ).start()

    def finish_block(other, step, both_peaks):
        rows = rows_of(other, BLOCK)
        out_a, tan_a = block_values(0, both_peaks[0])
        out_b, tan_b = block_values(1, both_peaks[1])
        heads_out[rows, :] = jnp.where(low, out_a, out_b).astype(jnp.bfloat16)
        heads_tan[rows, :] = jnp.where(low, tan_a, tan_b).astype(jnp.bfloat16)
        for side in range(2):
            hand_back(2 * other + side)
        heads_in[rows, lanes_of(place)] = heads_out[rows, :]

        @pl.when(step < EARLY)
        def _():
            hand_over(rows)


    def body(step, carry):
        other = jnp.bitwise_xor(chip, step)

        part = q_in.at[pl.ds(0, 4 * TOK), :]
        remote(part, part, send.at[4], recv_q.at[other], (dp, sibling)).wait_recv()

        @pl.when(step == 2)
        def _():
            forward_weight_rows(dp)

        @pl.when(step == 4)
        def _():
            forward_weight_rows(second)

        @pl.when(step == 6)
        def _():
            forward_weight_rows(third)

        rows = rows_of(other, BLOCK)
        peak_a = block_scores(rows, 0)
        peak_b = block_scores(rows, 1)
        finish_block(other, step, (peak_a, peak_b))
        return carry

    finish_block(chip, jnp.int32(0), first_peaks)
    lax.fori_loop(1, GROUP // 2, body, 0)

    for slot, (held, first) in enumerate(((heads_out, 0), (heads_tan, TOK))):
        pltpu.make_async_copy(
            held.at[rows_of(me, TOK), :], ret.at[pl.ds(first, TOK), lanes_of(heads_of(me))],
            back_local.at[slot],
        ).wait()


    def hand_rest(step, carry):
        hand_over(rows_of(jnp.bitwise_xor(chip, step), BLOCK))
        return carry

    lax.fori_loop(EARLY, GROUP // 2, hand_rest, 0)
    def handed(step):
        return remote(
            heads_out, heads_in.at[:, lanes_of(place)], a_send.at[step], a_recv.at[step],
            (dp, jnp.bitwise_xor(me, 4 * step)),
        )

    def forward(step):
        held = heads_in.at[:, lanes_of(2 * jnp.bitwise_xor(x, step) + core)]
        return remote(held, held, f_send.at[step], f_recv.at[step], (dp, sibling))

    forward(0).start()
    forward_weight_rows(fourth)
    part = w_in.at[pl.ds(0, (GROUP - 1) * half_rows), :]
    remote(part, part, w_send, w_forward, (dp, sibling)).wait_recv()
    load_latents.wait()
    load_tan.wait()
    back = remote(
        ret.at[pl.ds(0, BACK_ROWS), :], ret.at[pl.ds(0, BACK_ROWS), :],
        back_send, back_recv, (dp, sibling),
    )
    back.wait_recv()

    gate = modulation[0, 0:1, :].astype(jnp.float32)
    gate_tan = modulation[0, 1:2, :].astype(jnp.float32)
    square = jnp.zeros((TOK, LANES), jnp.float32)
    for chunk in range(FEAT // WCHUNK):
        span = slice(chunk * WCHUNK, (chunk + 1) * WCHUNK)
        both = dot(ret[...], w_in[:, span])
        plain = both[:TOK]
        blended_out[0, :, span] = (
            latents[0, :, span].astype(jnp.float32) + gate[:, span] * plain
        ).astype(jnp.bfloat16)
        value = (
            latent_tan[0, :, span].astype(jnp.float32)
            + gate_tan[:, span] * plain
            + gate[:, span] * both[TOK:]
        )
        tangent[:, span] = value
        tan_out[0, :, span] = value.astype(jnp.bfloat16)
        power = value * value
        for column in range(WCHUNK // LANES):
            square = square + power[:, column * LANES : (column + 1) * LANES]
    store_blended = pltpu.make_async_copy(blended_out, blended_hbm, o_sem.at[0])
    store_blended.start()
    store_tan = pltpu.make_async_copy(tan_out, tan_hbm, o_sem.at[1])
    store_tan.start()
    length = jnp.sqrt(jnp.sum(square, axis=1, keepdims=True))
    scale = 1.0 / (length + 0.1)
    for chunk in range(FEAT // WCHUNK):
        span = slice(chunk * WCHUNK, (chunk + 1) * WCHUNK)
        rounded = (gate[:, span] * tangent[:, span] * scale).astype(jnp.bfloat16)
        direction[:, span] = rounded

    def turn(part):
        return (part + z_hi) % 2

    def send_direction(part):
        def one(step, carry):
            partner = jnp.bitwise_xor(me, step)
            remote(
                direction.at[:, lanes_of(4 * (partner // 4) + 2 * (partner % 2) + turn(part))],
                dir_in.at[rows_of(me, TOK), pl.ds(part * LANES, LANES)],
                d_send, d_recv.at[part], (dp, partner),
            ).start()
            return carry

        lax.fori_loop(1, GROUP, one, 0)
        keep_part(part).start()

    def keep_part(part):
        return pltpu.make_async_copy(
            direction.at[:, lanes_of(4 * x + 2 * core + turn(part))],
            dir_in.at[rows_of(me, TOK), pl.ds(part * LANES, LANES)],
            d_local.at[part],
        )

    def finish_part(part):
        span = slice(part * LANES, (part + 1) * LANES)
        keep_part(part).wait()
        others = dir_in.at[pl.ds(0, (GROUP - 1) * TOK), pl.ds(0, LANES)]
        remote(others, others, d_send, d_recv.at[part], (dp, sibling)).wait_recv()
        partial[span, :] = dot_columns(dir_in[:, span], heads_in[...]).astype(jnp.bfloat16)

        def send_rows(step, carry):
            other = jnp.bitwise_xor(y, step)
            for side in range(2):
                remote(
                    partial.at[pl.ds(part * LANES, LANES), lanes_of(block_of(other, side))],
                    stage_in.at[part, step - 1, side], h_send, h_recv.at[part],
                    (jnp.bitwise_xor(dp, step), me),
                ).start()
            return carry

        lax.fori_loop(1, 4, send_rows, 0)

    def block_of(row, side):
        return 2 * lax.rem(row + 8 - z - 2 * side, 4) + side

    def reduce_part(part):
        held = stage_in.at[part]
        remote(held, held, h_send, h_recv.at[part], (dp, sibling)).wait_recv()
        owner = 4 * x + 2 * core + turn(part)
        for side in range(2):
            block = block_of(y, side)
            total = partial[part * LANES : (part + 1) * LANES, lanes_of(block)].astype(jnp.float32)
            for step in range(3):
                total = total + stage_in[part, step, side].astype(jnp.float32)
            middle[part, side] = total.astype(jnp.bfloat16)
            row = 4 * (block // 2) + y
            to_self = jnp.logical_and(row == dp, owner == me)

            @pl.when(jnp.logical_not(to_self))
            def _():
                remote(
                    middle.at[part, side], shares.at[z_hi], g_send, g_recv, (row, owner)
                ).start()

            @pl.when(to_self)
            def _():
                pltpu.make_async_copy(middle.at[part, side], shares.at[z_hi], g_local).start()

    for part in range(PARTS):
        send_direction(part)
    for step in (1, 3, 2):
        handed(step).wait_recv()
        forward(step).start()
    for step in range(4):
        forward(step).wait_recv()
    for part in range(PARTS):
        finish_part(part)
    for part in range(PARTS):
        reduce_part(part)

    @pl.when(grad_self)
    def _():
        part = shares.at[pl.ds(0, SUMS - 1)]
        pltpu.make_async_copy(shares.at[0], shares.at[1], g_local).wait()
        whole = remote(part, part, g_send, g_recv, (dp, sibling))
        whole.wait_send()
        whole.wait_recv()

    @pl.when(jnp.logical_not(grad_self))
    def _():
        whole = remote(shares, shares, g_send, g_recv, (dp, sibling))
        whole.wait_send()
        whole.wait_recv()

    store_blended.wait()
    store_tan.wait()
    total = shares[0].astype(jnp.float32)
    for sample in range(1, SUMS):
        total = total + shares[sample].astype(jnp.float32)
    grad_out[...] = -2.0 * total.T

    remote(stage_in, stage_in, h_send, h_recv.at[0], (dp, sibling)).wait_send()
    others = dir_in.at[pl.ds(0, (GROUP - 1) * TOK), :]
    remote(others, others, d_send, d_recv.at[0], (dp, sibling)).wait_send()
    for step in (1, 3, 2):
        handed(step).wait_send()
    for step in range(4):
        forward(step).wait_send()
    back.wait_send()
    part = w_in.at[pl.ds(0, 2 * (GROUP - 1) * half_rows), :]
    remote(part, part, w_send, w_forward, (dp, sibling)).wait_send()
    all_keys(3, vt_in).wait_send()
    for slot, (src, dst) in enumerate(queried):
        part = dst.at[pl.ds(0, (GROUP - 1) * TOK), :]
        remote(part, part, send.at[4 + slot], recv_q.at[0], (dp, sibling)).wait_send()


def whole(*args):
    half = jnp.bfloat16
    dma = pltpu.SemaphoreType.DMA
    vmem = pltpu.VMEM
    return pl.pallas_call(
        whole_kernel,
        out_shape=[
            jax.ShapeDtypeStruct((1, TOK, FEAT), half),
            jax.ShapeDtypeStruct((1, TOK, FEAT), half),
            jax.ShapeDtypeStruct((LANES, LANES), jnp.float32),
        ],
        in_specs=[ANY] * 8 + [VM, ANY],
        out_specs=[ANY, ANY, VM],
        scratch_shapes=[
            vmem((TOKENS, LANES), half),
            vmem((KEYS, LANES), half),
            vmem((KEYS, LANES), half),
            vmem((TOKENS, LANES), half),
            vmem((KEYS, LANES), half),
            vmem((KEYS, LANES), half),
            vmem((KEYS, 2 * LANES), half),
            vmem((KEYS, 2 * LANES), half),
            vmem((KEYS, 2 * LANES), half),
            vmem((2, 2 * BLOCK, 2 * LANES), half),
            vmem((2, 2 * BLOCK, KEYS), jnp.float32),
            vmem((TOKENS, LANES), half),
            vmem((TOKENS, LANES), half),
            vmem((2 * TOK, FEAT), half),
            vmem((FEAT, FEAT), half),
            vmem((1, TOK, FEAT), half),
            vmem((1, TOK, FEAT), half),
            vmem((TOK, FEAT), jnp.float32),
            vmem((TOK, FEAT), half),
            vmem((TOKENS, HALF_HEADS * LANES), half),
            vmem((TOKENS, PARTS * LANES), half),
            vmem((PARTS * LANES, HALF_HEADS * LANES), half),
            vmem((SUMS, LANES, LANES), half),
            dma((6,)), dma((4,)), dma((GROUP // 2,)), dma((6,)), dma, dma, dma((2,)),
            dma, dma((GROUP,)), dma, dma, dma((2,)),
            dma, dma((4,)), dma((4,)), dma((4,)), dma((4,)), dma, dma((PARTS,)), dma((PARTS,)),
            dma, dma, dma,
            vmem((1, TOK, FEAT), half), vmem((1, TOK, FEAT), half), dma((2,)),
            vmem((PARTS, 3, 2, LANES, LANES), half), vmem((PARTS, 2, LANES, LANES), half),
            dma, dma((PARTS,)),
        ],
        compiler_params=pltpu.CompilerParams(
            collective_id=0, has_side_effects=True, vmem_limit_bytes=56 * 2**20
        ),
        name="whole",
        cost_estimate=pl.CostEstimate(
            flops=10_500_000_000, bytes_accessed=20_000_000, transcendentals=9_437_184
        ),
    )(*args)


def finish_kernel(*refs):
    count = len(refs) // 2
    for index in range(count):
        refs[count + index][...] = refs[index][...]


def finish(arrays):
    return tuple(
        pl.pallas_call(
            finish_kernel,
            out_shape=[jax.ShapeDtypeStruct(array.shape, array.dtype) for array in arrays],
            in_specs=[VM] * len(arrays),
            out_specs=[VM] * len(arrays),
            name="finish",
        )(*arrays)
    )


def shards(
    queries, key_vectors, value_vectors, query_tangent, key_tangent, value_tangent,
    latents, latent_tangent, modulation, out_weight,
):
    return finish(
        whole(
            queries, key_vectors, value_vectors, query_tangent, key_tangent, value_tangent,
            latents, latent_tangent, modulation, out_weight,
        )
    )


def solution(mesh):
    tokens = P("dp", "seq", None)
    in_specs = (tokens,) * 8 + (P("dp", None, None), P("dp", None))
    out_specs = (tokens, tokens, P("dp", "seq"))
    return jax.shard_map(
        shards, mesh=mesh, in_specs=in_specs, out_specs=out_specs, check_vma=False
    )
```
